32 devices in a mesh: groups: 2 (over x), tm: 8 (over z, y), mode: 2 (over core).
Axes of the slice: x: 2, y: 2, z: 4, core: 2. Of those that a mesh axis runs over, the one named last changes fastest.
Arguments:
- coupling: float32 [16, 1024, 1024], P(('groups', 'tm'), None, 'mode'), parts along dimension 0, may hold values from -0.02734375 to 0.02734375
- decay: float32 [16, 1024], P(('groups', 'tm'), 'mode'), parts along dimension 0, may hold values from 0.39 to 1, as said below
- block_mask: int32 [8, 8], replicated, may hold values 0 or 1
- forcing: float32 [16, 1024, 128], P(('groups', 'tm'), 'mode'), parts along dimension 0, may hold values from -6 to 6
- misfit: float32 [16, 1024, 128], P(('groups', 'tm'), 'mode'), parts along dimension 0, may hold values from -6 to 6
Outputs:
- state: float32 [16, 1024, 128], P(('groups', 'tm'), 'mode'), parts along dimension 0
- adjoint: float32 [16, 1024, 128], P(('groups', 'tm'), 'mode'), parts along dimension 0
- grad_coupling: float32 [16, 1024, 1024], P(('groups', 'tm'), None, 'mode'), parts along dimension 0
- grad_decay: float32 [16, 1024], P(('groups', 'tm'), 'mode'), parts along dimension 0
The draws below stay inside these ranges and needn't reach their ends.
There are 2 independent parts, one for each index of `groups`. The reference program is written for one: setup_inputs(seed, part) draws one part's arguments, and reference() takes and returns one part's arrays. A program takes and returns all parts, laid end to end along the dimension named above; an argument that names none is the same for every part. Nothing has to cross between parts.
Inputs may be any that keep to these rules, and one draw needn't show every extreme that they name: `decay`: each mode keeps a share of its heat over a step that varies from mode to mode and step to step; at a few steps of the cycle every mode loses a larger share.
All inputs are finite; a program needn't handle non-finite values.
Results may differ from the reference program's by a relative error of at most 0.0003.
Values sent between devices are 32-bit elements; how exact they have to be, the bound alone decides.
A program may use at most 128 MiB of HBM per device.

```python
import math
import jax
import jax.numpy as jnp
from jax import lax

MODES = 1024
BLOCK = 128
SCEN = 128
SPIN = 4
STEPS = 8
LEVELS = 3
NBLK = 8


def draw_decay(key, part):
    first, second, third, fourth = jax.random.split(key, 4)
    life = jnp.exp(jax.random.uniform(first, (MODES,), jnp.float32, math.log(6.0), math.log(160.0)))
    factor = jnp.exp(jax.random.uniform(second, (STEPS, MODES), jnp.float32, math.log(0.7), math.log(1.4)))
    rate = jnp.exp(-1.0 / (life[None, :] * factor))
    places = jax.random.randint(third, (3,), 0, STEPS)
    hit = jnp.any(jnp.arange(STEPS)[:, None] == places[None, :], axis=1)
    loss = jax.random.uniform(fourth, (STEPS,), jnp.float32, 0.5, 0.8)
    scale = jnp.where(hit, loss, 1.0)
    return (rate * scale[:, None]).astype(jnp.float32)


def touch_ends(entries, rng, smallest, high):
    index_at = [jax.random.randint(jax.random.fold_in(rng, axis), (), 0, length) for axis, length in enumerate(entries.shape)]
    longest = entries.shape.index(max(entries.shape))
    next_to = index_at[:longest] + [(index_at[longest] + 1) % entries.shape[longest]] + index_at[longest + 1:]
    return entries.at[tuple(index_at)].set(smallest).at[tuple(next_to)].set(high)


def levels(key, shape, cuts, least, top_value):
    gain = 1.0
    for axis_at, blocks in cuts:
        draws = jax.random.uniform(jax.random.fold_in(jax.random.fold_in(key, 6), axis_at), (blocks,), jnp.float32, least / len(cuts), top_value / len(cuts))
        gain = gain * jnp.repeat(jnp.exp(draws), shape[axis_at] // blocks).reshape((-1,) + (1,) * (len(shape) - 1 - axis_at))
    return gain


def scatter_about(key, shape, spread, bound, cuts=(), held_as=jnp.bfloat16):
    result = spread * jax.random.normal(key, shape, jnp.float32)
    if cuts:
        result = result * levels(key, shape, cuts, -0.22, 0.18)
    return jnp.clip(result, -bound, bound).astype(held_as)


def setup_inputs(seed: int = 0, part: int = 0) -> dict:
    arg_keys = jax.random.split(jax.random.key(seed), 6)
    part_splits = jax.random.split(jax.random.fold_in(arg_keys[5], part), 6)
    coupling = scatter_about(part_splits[0], (STEPS, MODES, MODES), (MODES * 44) ** -0.5, 0.02734375, ((0, 8), (2, 2)), jnp.float32)
    decay = draw_decay(jax.random.fold_in(jax.random.fold_in(arg_keys[5], part), 71), part)
    block_mask = touch_ends((jax.random.randint(arg_keys[2], (NBLK, NBLK), 0, 2) < 1).astype(jnp.int32), jax.random.fold_in(arg_keys[2], 1), 0, 1)
    forcing = scatter_about(part_splits[3], (STEPS, MODES, SCEN), 1.0, 6.0, ((0, 8), (1, 2)), jnp.float32)
    misfit = scatter_about(part_splits[4], (STEPS, MODES, SCEN), 1.0, 6.0, ((0, 8), (1, 2)), jnp.float32)
    return dict(coupling=coupling, decay=decay, block_mask=block_mask, forcing=forcing, misfit=misfit)


def mat(a, b):
    return jnp.einsum("tij,tjk->tik", a, b, precision=lax.Precision.HIGHEST)


def tmat(a, b):
    return jnp.einsum("tji,tjk->tik", a, b, precision=lax.Precision.HIGHEST)


def reference(coupling, decay, block_mask, forcing, misfit):
    pattern = jnp.repeat(jnp.repeat(block_mask.astype(jnp.float32), BLOCK, 0), BLOCK, 1)
    eye = jnp.eye(MODES, dtype=jnp.float32)
    matrix = coupling * pattern[None] + eye[None] * decay[:, None, :]
    vector = forcing
    stored = []
    for level in range(LEVELS):
        stored.append(matrix)
        shifted_matrix = jnp.roll(matrix, 2 ** level, axis=0)
        shifted_vector = jnp.roll(vector, 2 ** level, axis=0)
        vector = mat(matrix, shifted_vector) + vector
        matrix = mat(matrix, shifted_matrix)
    cycle = matrix
    state = vector
    for turn in range(SPIN - 1):
        state = mat(cycle, state) + vector
    carried = misfit
    for level in range(LEVELS):
        back = tmat(stored[level], carried)
        carried = carried + jnp.roll(back, -(2 ** level), axis=0)
    adjoint = carried
    for turn in range(SPIN - 1):
        adjoint = tmat(cycle, adjoint) + carried
    prior = jnp.roll(state, 1, axis=0)
    outer = jnp.einsum("tis,tjs->tij", adjoint, prior, precision=lax.Precision.HIGHEST)
    grad_coupling = pattern[None] * outer / SCEN
    grad_decay = jnp.sum(adjoint * prior, axis=2) / SCEN
    return state, adjoint, grad_coupling, grad_decay
```

```python
import jax
import jax.numpy as jnp
from jax import lax
from jax.sharding import PartitionSpec as P

BLOCK = 128
SCEN = 128
SPIN = 4
CHUNKS = 2


def passed_along(value, axis, steps):
    count = lax.axis_size(axis)
    pairs = [(source, (source + steps) % count) for source in range(count)]
    return lax.ppermute(value, axis, pairs)


def product(left, right):
    return jnp.dot(left, right, precision=lax.Precision.HIGH, preferred_element_type=jnp.float32)


def tproduct(left, right):
    return lax.dot_general(
        left,
        right,
        (((0,), (0,)), ((), ())),
        precision=lax.Precision.HIGH,
        preferred_element_type=jnp.float32,
    )


def full_rows(vector):
    return lax.all_gather(vector, "mode", axis=0, tiled=True)


def summed_rows(panel, rows):
    partial = product(panel, rows)
    half = partial.shape[0] // 2
    mine = lax.axis_index("mode")
    own = lax.dynamic_slice_in_dim(partial, mine * half, half, 0)
    other = lax.dynamic_slice_in_dim(partial, (1 - mine) * half, half, 0)
    return own + lax.ppermute(other, "mode", [(0, 1), (1, 0)])


def leads(step, count):
    low = step % (count // 2)
    return (step < count // 2) == ((low // 2) % 2 == 0)


def per_device(coupling, decay, block_mask, forcing, misfit):
    panel = coupling.shape[2]
    modes = coupling.shape[1]
    count = lax.axis_size("tm")
    start = lax.axis_index("mode") * panel
    pattern = jnp.repeat(jnp.repeat(block_mask.astype(jnp.float32), BLOCK, 0), BLOCK, 1)
    mask_panel = lax.dynamic_slice_in_dim(pattern, start, panel, 1)
    row_index = lax.broadcasted_iota(jnp.int32, (modes, panel), 0)
    col_index = lax.broadcasted_iota(jnp.int32, (modes, panel), 1) + start
    diagonal = jnp.where(row_index == col_index, decay[0][None, :], 0.0)
    width = panel // CHUNKS
    matrix = coupling[0] * mask_panel + diagonal
    pieces = [matrix[:, i * width:(i + 1) * width] for i in range(CHUNKS)]
    vector = forcing[0]
    carried = misfit[0]
    levels = count.bit_length() - 1
    for level in range(levels - 1):
        recv_vector = passed_along(vector, "tm", 2**level)
        recv_pieces = [passed_along(piece, "tm", 2**level) for piece in pieces]
        left = lax.all_gather(matrix, "mode", axis=1, tiled=True)
        back = tproduct(matrix, full_rows(carried))
        carried = carried + passed_along(back, "tm", -(2**level))
        vector = summed_rows(matrix, recv_vector) + vector
        vector, carried, left = lax.optimization_barrier((vector, carried, left))
        pieces = [product(left, piece) for piece in recv_pieces]
        matrix = jnp.concatenate(pieces, axis=1)
    half = count // 2
    here = [step for step in range(count) if leads(step, count)]
    to_lead = [((step + half) % count, step) for step in here]
    from_lead = [(step, (step + half) % count) for step in here]
    index = lax.axis_index("tm")
    is_lead = (index < half) == (((index % half) // 2) % 2 == 0)
    recv_vector = lax.ppermute(vector, "tm", to_lead)
    recv_pieces = [lax.ppermute(piece, "tm", to_lead) for piece in pieces]
    left = lax.all_gather(matrix, "mode", axis=1, tiled=True)
    back = tproduct(matrix, full_rows(carried))
    gathered = carried + lax.ppermute(back, "tm", to_lead)
    forced = summed_rows(matrix, recv_vector) + vector
    forced, gathered, left = lax.optimization_barrier((forced, gathered, left))
    cycle = jnp.concatenate([product(left, piece) for piece in recv_pieces], axis=1)
    add_state = jnp.concatenate([forced, jnp.zeros_like(forced)], axis=1)
    add_adjoint = jnp.concatenate([gathered, jnp.zeros_like(gathered)], axis=1)
    state = jnp.concatenate([forced, vector], axis=1)
    adjoint = jnp.concatenate([gathered, carried], axis=1)
    for turn in range(SPIN - 1):
        short_state, short_adjoint = state[:, :SCEN], adjoint[:, :SCEN]
        state = summed_rows(cycle, state) + add_state
        adjoint = tproduct(cycle, full_rows(adjoint)) + add_adjoint
    short_state = short_state + state[:, SCEN:]
    short_adjoint = short_adjoint + adjoint[:, SCEN:]
    recv_state = lax.ppermute(short_state, "tm", from_lead)
    back = tproduct(matrix, full_rows(short_adjoint))
    recv_adjoint = lax.ppermute(back, "tm", from_lead)
    other_state = summed_rows(matrix, recv_state) + vector
    state = jnp.where(is_lead, state[:, :SCEN], other_state)
    adjoint = jnp.where(is_lead, adjoint[:, :SCEN], carried + recv_adjoint)
    whole_adjoint = full_rows(adjoint)
    prior = passed_along(state, "tm", 1)
    outer = lax.dot_general(
        whole_adjoint,
        prior,
        (((1,), (1,)), ((), ())),
        precision=lax.Precision.HIGH,
        preferred_element_type=jnp.float32,
    )
    grad_coupling = mask_panel * outer / SCEN
    grad_decay = jnp.sum(adjoint * prior, axis=1) / SCEN
    return (state[None], adjoint[None], grad_coupling[None], grad_decay[None])


def solution(mesh):
    placed = (
        P(("groups", "tm"), None, "mode"),
        P(("groups", "tm"), "mode"),
        P(),
        P(("groups", "tm"), "mode", None),
        P(("groups", "tm"), "mode", None),
    )
    return jax.shard_map(
        per_device,
        mesh=mesh,
        in_specs=placed,
        out_specs=(
            P(("groups", "tm"), "mode", None),
            P(("groups", "tm"), "mode", None),
            P(("groups", "tm"), None, "mode"),
            P(("groups", "tm"), "mode"),
        ),
        check_vma=False,
    )
```

```python
import jax
import jax.numpy as jnp
from jax import lax
from jax.sharding import PartitionSpec as P

BLOCK = 128
SCEN = 128
SPIN = 4
CUTS = (1,)


def passed_along(value, axis, steps):
    count = lax.axis_size(axis)
    pairs = [(source, (source + steps) % count) for source in range(count)]
    return lax.ppermute(value, axis, pairs)


def product(left, right):
    return jnp.dot(left, right, precision=lax.Precision.HIGH, preferred_element_type=jnp.float32)


def tproduct(left, right):
    return lax.dot_general(
        left,
        right,
        (((0,), (0,)), ((), ())),
        precision=lax.Precision.HIGH,
        preferred_element_type=jnp.float32,
    )


def full_rows(vector):
    return lax.all_gather(vector, "mode", axis=0, tiled=True)


def swapped(value):
    return lax.ppermute(value, "mode", [(0, 1), (1, 0)])


def in_order(left, pieces):
    done = []
    for piece in pieces:
        if done:
            done[-1], piece = lax.optimization_barrier((done[-1], piece))
        done.append(product(left, piece))
    return done


def leads(step, count):
    low = step % (count // 2)
    return (step < count // 2) == ((low // 2) % 2 == 0)


def per_device(coupling, decay, block_mask, forcing, misfit):
    panel = coupling.shape[2]
    modes = coupling.shape[1]
    count = lax.axis_size("tm")
    start = lax.axis_index("mode") * panel
    pattern = jnp.repeat(jnp.repeat(block_mask.astype(jnp.float32), BLOCK, 0), BLOCK, 1)
    mask_panel = lax.dynamic_slice_in_dim(pattern, start, panel, 1)
    row_index = lax.broadcasted_iota(jnp.int32, (modes, panel), 0)
    col_index = lax.broadcasted_iota(jnp.int32, (modes, panel), 1) + start
    diagonal = jnp.where(row_index == col_index, decay[0][None, :], 0.0)
    mode = lax.axis_index("mode")
    bounds = [0] + [panel * cut // 4 for cut in CUTS] + [panel]
    matrix = coupling[0] * mask_panel + diagonal
    pieces = [matrix[:, low:high] for low, high in zip(bounds[:-1], bounds[1:])]
    vector = forcing[0]
    carried = misfit[0]
    levels = count.bit_length() - 1
    for level in range(levels - 1):
        recv_pieces = [passed_along(piece, "tm", 2**level) for piece in pieces]
        recv_vector = passed_along(vector, "tm", 2**level)
        left = lax.all_gather(matrix, "mode", axis=1, tiled=True)
        own_rows = lax.dynamic_slice_in_dim(left, start, panel, 0)
        back = tproduct(matrix, full_rows(carried))
        vector = product(own_rows, full_rows(recv_vector)) + vector
        carried = carried + passed_along(back, "tm", -(2**level))
        vector, carried, left = lax.optimization_barrier((vector, carried, left))
        pieces = in_order(left, recv_pieces)
        matrix = jnp.concatenate(pieces, axis=1)
    half = count // 2
    here = [step for step in range(count) if leads(step, count)]
    to_lead = [((step + half) % count, step) for step in here]
    from_lead = [(step, (step + half) % count) for step in here]
    index = lax.axis_index("tm")
    is_lead = (index < half) == (((index % half) // 2) % 2 == 0)
    recv_pieces = [lax.ppermute(piece, "tm", to_lead) for piece in pieces]
    recv_vector = lax.ppermute(vector, "tm", to_lead)
    left = lax.all_gather(matrix, "mode", axis=1, tiled=True)
    own_rows = lax.dynamic_slice_in_dim(left, start, panel, 0)
    back = tproduct(matrix, full_rows(carried))
    gathered = carried + lax.ppermute(back, "tm", to_lead)
    forced = product(own_rows, full_rows(recv_vector)) + vector
    first = mode == 0
    forced, gathered, left = lax.optimization_barrier((forced, gathered, left))
    state = jnp.where(first, full_rows(forced), full_rows(vector))
    adjoint = jnp.where(first, full_rows(gathered), full_rows(carried))
    add_state = jnp.where(first, state, 0.0)
    add_adjoint = jnp.where(first, adjoint, 0.0)
    own = in_order(left, recv_pieces)
    other = [swapped(piece) for piece in own]
    cycle = jnp.where(first, jnp.concatenate(own + other, axis=1), jnp.concatenate(other + own, axis=1))
    for turn in range(SPIN - 1):
        short_state, short_adjoint = state, adjoint
        state = product(cycle, state) + add_state
        adjoint = tproduct(cycle, adjoint) + add_adjoint
    ends = jnp.concatenate([state, short_state, adjoint, short_adjoint], axis=1)
    kept = lax.dynamic_slice_in_dim(ends, start, panel, 0)
    came = swapped(lax.dynamic_slice_in_dim(ends, panel - start, panel, 0))
    sums = jnp.where(first, kept, came)
    powers = jnp.where(first, came, kept)
    state, adjoint = sums[:, :SCEN], sums[:, 2 * SCEN:3 * SCEN]
    short_state = sums[:, SCEN:2 * SCEN] + powers[:, :SCEN]
    short_adjoint = sums[:, 3 * SCEN:] + powers[:, 2 * SCEN:3 * SCEN]
    recv_state = lax.ppermute(short_state, "tm", from_lead)
    back = tproduct(matrix, full_rows(short_adjoint))
    recv_adjoint = lax.ppermute(back, "tm", from_lead)
    other_state = product(own_rows, full_rows(recv_state)) + vector
    state = jnp.where(is_lead, state, other_state)
    adjoint = jnp.where(is_lead, adjoint, carried + recv_adjoint)
    whole_adjoint = full_rows(adjoint)
    prior = passed_along(state, "tm", 1)
    outer = lax.dot_general(
        whole_adjoint,
        prior,
        (((1,), (1,)), ((), ())),
        precision=lax.Precision.HIGH,
        preferred_element_type=jnp.float32,
    )
    grad_coupling = mask_panel * outer / SCEN
    grad_decay = jnp.sum(adjoint * prior, axis=1) / SCEN
    return (state[None], adjoint[None], grad_coupling[None], grad_decay[None])


def solution(mesh):
    placed = (
        P(("groups", "tm"), None, "mode"),
        P(("groups", "tm"), "mode"),
        P(),
        P(("groups", "tm"), "mode", None),
        P(("groups", "tm"), "mode", None),
    )
    return jax.shard_map(
        per_device,
        mesh=mesh,
        in_specs=placed,
        out_specs=(
            P(("groups", "tm"), "mode", None),
            P(("groups", "tm"), "mode", None),
            P(("groups", "tm"), None, "mode"),
            P(("groups", "tm"), "mode"),
        ),
        check_vma=False,
    )
```

```python
import jax
import jax.numpy as jnp
from jax import lax
from jax.sharding import PartitionSpec as P

BLOCK = 128
SCEN = 128
SPIN = 4
CHUNKS = 2


def passed_along(value, axis, steps):
    count = lax.axis_size(axis)
    pairs = [(source, (source + steps) % count) for source in range(count)]
    return lax.ppermute(value, axis, pairs)


def product(left, right):
    return jnp.dot(left, right, precision=lax.Precision.HIGH, preferred_element_type=jnp.float32)


def tproduct(left, right):
    return lax.dot_general(
        left,
        right,
        (((0,), (0,)), ((), ())),
        precision=lax.Precision.HIGH,
        preferred_element_type=jnp.float32,
    )


def full_rows(vector):
    return lax.all_gather(vector, "mode", axis=0, tiled=True)


def summed_rows(panel, rows):
    partial = product(panel, rows)
    half = partial.shape[0] // 2
    mine = lax.axis_index("mode")
    own = lax.dynamic_slice_in_dim(partial, mine * half, half, 0)
    other = lax.dynamic_slice_in_dim(partial, (1 - mine) * half, half, 0)
    return own + lax.ppermute(other, "mode", [(0, 1), (1, 0)])


def in_order(left, pieces):
    done = []
    for piece in pieces:
        if done:
            done[-1], piece = lax.optimization_barrier((done[-1], piece))
        done.append(product(left, piece))
    return done


def leads(step, count):
    low = step % (count // 2)
    return (step < count // 2) == ((low // 2) % 2 == 0)


def per_device(coupling, decay, block_mask, forcing, misfit):
    panel = coupling.shape[2]
    modes = coupling.shape[1]
    count = lax.axis_size("tm")
    start = lax.axis_index("mode") * panel
    pattern = jnp.repeat(jnp.repeat(block_mask.astype(jnp.float32), BLOCK, 0), BLOCK, 1)
    mask_panel = lax.dynamic_slice_in_dim(pattern, start, panel, 1)
    row_index = lax.broadcasted_iota(jnp.int32, (modes, panel), 0)
    col_index = lax.broadcasted_iota(jnp.int32, (modes, panel), 1) + start
    diagonal = jnp.where(row_index == col_index, decay[0][None, :], 0.0)
    width = panel // CHUNKS
    matrix = coupling[0] * mask_panel + diagonal
    pieces = [matrix[:, i * width:(i + 1) * width] for i in range(CHUNKS)]
    vector = forcing[0]
    carried = misfit[0]
    levels = count.bit_length() - 1
    half = count // 2
    here = [step for step in range(count) if leads(step, count)]
    to_lead = [((step + half) % count, step) for step in here]
    from_lead = [(step, (step + half) % count) for step in here]
    index = lax.axis_index("tm")
    is_lead = (index < half) == (((index % half) // 2) % 2 == 0)
    last_matrix = recv_vector = recv_back = None
    for level in range(levels):
        shift = 2**level
        last = level == levels - 1
        forward = to_lead if last else [(step, (step + shift) % count) for step in range(count)]
        backward = to_lead if last else [(step, (step - shift) % count) for step in range(count)]
        recv_pieces = [lax.ppermute(piece, "tm", forward) for piece in pieces]
        left = lax.all_gather(matrix, "mode", axis=1, tiled=True)
        if level:
            vector = summed_rows(last_matrix, recv_vector) + vector
            carried = carried + recv_back
        back = tproduct(matrix, full_rows(carried))
        left, vector, back = lax.optimization_barrier((left, vector, back))
        recv_vector = lax.ppermute(vector, "tm", forward)
        recv_back = lax.ppermute(back, "tm", backward)
        last_matrix = matrix
        pieces = in_order(left, recv_pieces)
        matrix = jnp.concatenate(pieces, axis=1)
    cycle, matrix = matrix, last_matrix
    forced = summed_rows(matrix, recv_vector) + vector
    gathered = carried + recv_back
    add_state = jnp.concatenate([forced, jnp.zeros_like(forced)], axis=1)
    add_adjoint = jnp.concatenate([gathered, jnp.zeros_like(gathered)], axis=1)
    state = jnp.concatenate([forced, vector], axis=1)
    adjoint = jnp.concatenate([gathered, carried], axis=1)
    for turn in range(SPIN - 1):
        short_state, short_adjoint = state[:, :SCEN], adjoint[:, :SCEN]
        state = summed_rows(cycle, state) + add_state
        adjoint = tproduct(cycle, full_rows(adjoint)) + add_adjoint
    short_state = short_state + state[:, SCEN:]
    short_adjoint = short_adjoint + adjoint[:, SCEN:]
    recv_state = lax.ppermute(short_state, "tm", from_lead)
    back = tproduct(matrix, full_rows(short_adjoint))
    recv_adjoint = lax.ppermute(back, "tm", from_lead)
    other_state = summed_rows(matrix, recv_state) + vector
    state = jnp.where(is_lead, state[:, :SCEN], other_state)
    adjoint = jnp.where(is_lead, adjoint[:, :SCEN], carried + recv_adjoint)
    whole_adjoint = full_rows(adjoint)
    prior = passed_along(state, "tm", 1)
    outer = lax.dot_general(
        whole_adjoint,
        prior,
        (((1,), (1,)), ((), ())),
        precision=lax.Precision.HIGH,
        preferred_element_type=jnp.float32,
    )
    grad_coupling = mask_panel * outer / SCEN
    grad_decay = jnp.sum(adjoint * prior, axis=1) / SCEN
    return (state[None], adjoint[None], grad_coupling[None], grad_decay[None])


def solution(mesh):
    placed = (
        P(("groups", "tm"), None, "mode"),
        P(("groups", "tm"), "mode"),
        P(),
        P(("groups", "tm"), "mode", None),
        P(("groups", "tm"), "mode", None),
    )
    return jax.shard_map(
        per_device,
        mesh=mesh,
        in_specs=placed,
        out_specs=(
            P(("groups", "tm"), "mode", None),
            P(("groups", "tm"), "mode", None),
            P(("groups", "tm"), None, "mode"),
            P(("groups", "tm"), "mode"),
        ),
        check_vma=False,
    )
```
